32 devices in a mesh: parts: 2 (over x), wide: 16 (over z, y, core).
Axes of the slice: x: 2, y: 2, z: 4, core: 2. Of those that a mesh axis runs over, the one named last changes fastest.
Arguments:
- embeddings: bfloat16 [16384, 1024], P(('parts', 'wide')), parts along dimension 0, may hold values from -6 to 6
- cluster_id: int32 [16384, 1], P(('parts', 'wide')), parts along dimension 0, may hold values from 0 to 31; in each aligned block of 512 rows (0 to 511, 512 to 1023, ...) at most 32 rows name the same one
Outputs:
- similarity: float32 [16384], P(('parts', 'wide')), parts along dimension 0
The draws below stay inside these ranges and needn't reach their ends.
There are 2 independent parts, one for each index of `parts`. The reference program is written for one: setup_inputs(seed, part) draws one part's arguments, and reference() takes and returns one part's arrays. A program takes and returns all parts, laid end to end along the dimension named above; each array names one. Nothing has to cross between parts.
Inputs may be any that keep to these rules, and one draw needn't show every extreme that they name: The cluster of row r is cluster_id[r, 0]; cluster c belongs to device c // 2 of the wide axis. In each aligned block of 512 rows (the rows of one device) no cluster is named by more than 32 rows.
All inputs are finite; a program needn't handle non-finite values.
Results may differ from the reference program's by a relative error of at most 0.0013.
Values may be sent and summed in bfloat16 or wider, within the bound.
A program may use at most 64 MiB of HBM per device.

```python
import math
import jax
import jax.numpy as jnp
import numpy as np
from jax import lax

D = 1024
ROWS_DEV = 512
ROWS = 8192
CLUSTERS = 32
CAP = 32
SLOTS = 512


def level_of(own_key, extent, shards, smallest, largest):
    loudness, own = 1.0, jax.random.fold_in(own_key, 6)
    for dim, blocks in shards:
        heights = jnp.exp(jax.random.uniform(jax.random.fold_in(own, dim), (blocks,), jnp.float32, smallest / len(shards), largest / len(shards)))
        loudness = loudness * jnp.repeat(heights, extent[dim] // blocks).reshape([-1 if axis == dim else 1 for axis in range(len(extent))])
    return loudness


def shared_out(rng, own, number, rows, count, top, limit, slope):
    order = jax.random.permutation(rng, count)
    crowded, ordinary = load_shares(count, rows * top, limit, slope, True), load_shares(count, rows * top, limit, slope, False)
    places = jnp.arange(count)

    def named(tallies, offset_by):
        used = int((tallies > 0).sum())
        fixed = max(1, used // 4)
        passed = fixed + (places - fixed + offset_by * (used - fixed)) % max(1, count - fixed)
        return jnp.zeros((count,), jnp.int32).at[order[jnp.where(places < fixed, places, passed)]].set(jnp.asarray(tallies, jnp.int32))

    tallies = jnp.where(number % 4 == 0, named(crowded, number // 4), named(ordinary, number - number // 4 - 1))
    mixed = jax.random.permutation(jax.random.fold_in(own, 3), count)
    donor, taker = mixed[0:count // 2 * 2:2], mixed[1:count // 2 * 2:2]
    slack = jnp.minimum(tallies[donor] - 1, limit - tallies[taker]) // 2
    slack = jnp.where((donor == order[0]) | (taker == order[0]) | (tallies[taker] == 0), 0, jnp.maximum(slack, 0))
    passed = jax.random.randint(jax.random.fold_in(own, 4), (count // 2,), 0, 1 << 20) % (slack + 1)
    tallies = tallies.at[donor].add(-passed).at[taker].add(passed)
    items = jnp.searchsorted(jnp.cumsum(tallies), jnp.arange(rows * top), side="right").astype(jnp.int32)
    listing = items.reshape(top, rows).T
    listing = listing[jax.random.permutation(jax.random.fold_in(own, 1), rows)]
    offset_by = jax.random.randint(jax.random.fold_in(own, 2), (rows, 1), 0, top)
    return jnp.take_along_axis(listing, (jnp.arange(top)[None, :] + offset_by) % top, axis=1)


def load_shares(number_of, total, bound, lean, full):
    portions = [(1 << 20) // math.isqrt(rank ** lean) + 1 for rank in range(1, number_of + 1)]
    largest = bound if full else min(bound, max(-(-total // number_of), total * portions[0] // sum(portions)))
    least = 1 if total - largest >= number_of - 1 else 0
    holding, rest = [largest] + [least] * (number_of - 1), total - largest - least * (number_of - 1)
    while rest > 0:
        free = [i for i in range(1, number_of) if holding[i] < largest] or [i for i in range(1, number_of) if holding[i] < bound]
        mass, budget = sum([portions[i] for i in free]), rest
        for i in free:
            extra = min(bound - holding[i], max(1, budget * portions[i] // mass), rest)
            holding[i] = holding[i] + extra
            rest = rest - extra
    return np.array(holding)


def scatter_about(own_key, extent, scale, limit, cuts=(), held_as=jnp.bfloat16):
    gain = level_of(own_key, extent, cuts, -0.22, 0.18) if cuts else 1.0
    entries = jax.random.normal(own_key, extent, jnp.float32) * scale * gain
    return jnp.minimum(jnp.maximum(entries, -limit), limit).astype(held_as)


def setup_inputs(seed: int = 0, part: int = 0) -> dict:
    splits = jax.random.split(jax.random.key(seed), 3)
    own_keys = jax.random.split(jax.random.fold_in(splits[2], part), 3)
    embeddings = scatter_about(own_keys[0], (ROWS, D), 1.0, 6.0, ((0, 16),))
    cluster_id_keys = jax.random.split(jax.random.fold_in(own_keys[1], 1), ROWS // ROWS_DEV)
    cluster_id_turns = jax.random.permutation(jax.random.fold_in(own_keys[1], 3), ROWS // ROWS_DEV)
    cluster_id = jax.vmap(lambda own, number: shared_out(jax.random.fold_in(own_keys[1], 2), own, number, ROWS_DEV, CLUSTERS, 1, CAP, 2))(cluster_id_keys, cluster_id_turns).reshape((ROWS, 1))
    return dict(embeddings=embeddings, cluster_id=cluster_id)


def normalize(values):
    widened = values.astype(jnp.float32)
    scale = lax.rsqrt(lax.optimization_barrier(jnp.sum(widened * widened, axis=-1, keepdims=True)) + 1e-06)
    return (widened * scale).astype(jnp.bfloat16)

def reference(embeddings, cluster_id):
    unit = normalize(embeddings)
    cluster_ids = cluster_id[:, 0].astype(jnp.int32)
    order_rows = jnp.argsort(cluster_ids, stable=True).astype(jnp.int32)
    counts = jnp.zeros((CLUSTERS,), jnp.int32).at[cluster_ids].add(1)
    starts = (jnp.cumsum(counts) - counts).astype(jnp.int32)
    slot_range = jnp.arange(SLOTS, dtype=jnp.int32)

    def one_cluster(index):
        position = jnp.minimum(starts[index] + slot_range, ROWS - 1).astype(jnp.int32)
        members = unit[order_rows[position]]
        valid = slot_range < counts[index]
        gram = jnp.dot(members, members.T, preferred_element_type=jnp.float32)
        mask = (slot_range[None, :] < slot_range[:, None]) & valid[None, :]
        return lax.optimization_barrier(jnp.max(jnp.where(mask, gram, jnp.float32(-1.0)), axis=1))
    maxima = lax.map(one_cluster, jnp.arange(CLUSTERS, dtype=jnp.int32))
    sorted_ids = cluster_ids[order_rows]
    place_rank = (jnp.arange(ROWS, dtype=jnp.int32) - starts[sorted_ids]).astype(jnp.int32)
    values = maxima[sorted_ids, place_rank]
    return jnp.zeros((ROWS,), jnp.float32).at[order_rows].set(values)
```

```python
import functools

import jax
import jax.numpy as jnp
from jax import lax
from jax.experimental import pallas as pl
from jax.experimental.pallas import tpu as pltpu
from jax.sharding import PartitionSpec as P

CLUS_DEV = 2
LANES = 128
EMPTY = 4.0
FAR = 1 << 20


def normalize(values):
    widened = values.astype(jnp.float32)
    scale = lax.rsqrt(jnp.sum(widened * widened, axis=-1, keepdims=True) + 1e-06)
    return (widened * scale).astype(jnp.bfloat16)


def dispatch_kernel(
    n, cap, emb_ref, cid_ref, out_ref, unit, send, recv, res, ret,
    send_sem, recv_sem, back_send_sem, back_recv_sem,
):
    me = lax.axis_index("wide")
    rows, width = emb_ref.shape
    block = CLUS_DEV * cap
    slots = n * cap
    clusters = CLUS_DEV * n

    def peer(k):
        return lax.rem(me + k, n)

    barrier = pltpu.get_barrier_semaphore()

    def greet(k, carry):
        pl.semaphore_signal(
            barrier, inc=1, device_id={"wide": peer(k)}, device_id_type=pl.DeviceIdType.MESH
        )
        return carry

    lax.fori_loop(1, n, greet, 0)

    def unit_rows(t, carry):
        part = pl.ds(pl.multiple_of(t * 64, 64), 64)
        unit[part, :] = normalize(emb_ref[part, :])
        return carry

    lax.fori_loop(0, rows // 64, unit_rows, 0)
    cid = cid_ref[...]
    named = lax.broadcasted_iota(jnp.int32, (clusters, rows), 0) == cid
    before = lax.broadcasted_iota(jnp.int32, (rows, rows), 0) < lax.broadcasted_iota(
        jnp.int32, (rows, rows), 1
    )
    earlier = jnp.dot(
        jnp.where(named, 1.0, 0.0).astype(jnp.bfloat16),
        jnp.where(before, 1.0, 0.0).astype(jnp.bfloat16),
        preferred_element_type=jnp.float32,
    )
    rank = jnp.sum(jnp.where(named, earlier, 0.0), axis=0, keepdims=True).astype(jnp.int32)
    slot = cid * cap + rank

    pl.semaphore_wait(barrier, n - 1)

    def block_copy(k, place):
        return pltpu.make_async_remote_copy(
            src_ref=send.at[place],
            dst_ref=recv.at[me],
            send_sem=send_sem.at[k],
            recv_sem=recv_sem.at[k],
            device_id={"wide": peer(k)},
            device_id_type=pl.DeviceIdType.MESH,
        )

    order = sorted(range(n), key=lambda k: (abs(k - n // 2), k))
    group = 4
    for first in range(0, n, group):
        chosen = order[first:first + group]
        picks = jnp.concatenate(
            [
                jnp.where(
                    lax.broadcasted_iota(jnp.int32, (block, rows), 0) + peer(k) * block == slot,
                    1.0,
                    0.0,
                )
                for k in chosen
            ],
            axis=0,
        )
        packed = jnp.dot(
            picks.astype(jnp.bfloat16), unit[...], preferred_element_type=jnp.float32
        ).astype(jnp.bfloat16)
        filled = jnp.max(picks, axis=1, keepdims=True)
        head = packed[:, :LANES].astype(jnp.float32)
        marked = (lax.broadcasted_iota(jnp.int32, head.shape, 1) == 0) & (filled < 0.5)
        head = jnp.where(marked, EMPTY, head).astype(jnp.bfloat16)
        for i, k in enumerate(chosen):
            part = slice(i * block, (i + 1) * block)
            if k == 0:
                recv[me, :, :LANES] = head[part]
                recv[me, :, LANES:] = packed[part, LANES:]
            else:
                send[first + i, :, :LANES] = head[part]
                send[first + i, :, LANES:] = packed[part, LANES:]
                block_copy(k, first + i).start()

    def arrived(k, carry):
        pltpu.make_async_remote_copy(
            src_ref=send.at[0],
            dst_ref=recv.at[lax.rem(me + n - k, n)],
            send_sem=send_sem.at[k],
            recv_sem=recv_sem.at[k],
            device_id={"wide": peer(k)},
            device_id_type=pl.DeviceIdType.MESH,
        ).wait_recv()
        return carry

    lax.fori_loop(1, n, arrived, 0)

    step = 256
    for c in range(CLUS_DEV):
        for start in range(0, slots, step):
            top = start + step
            keys = recv[: top // cap, c * cap:(c + 1) * cap, :].reshape(top, width)
            queries = recv[start // cap:top // cap, c * cap:(c + 1) * cap, :].reshape(step, width)
            gram = lax.dot_general(
                keys, queries, (((1,), (1,)), ((), ())), preferred_element_type=jnp.float32
            )
            flag = keys[:, :LANES].astype(jnp.float32)[:, :1]
            position = lax.broadcasted_iota(jnp.int32, (top, 1), 0)
            position = jnp.where(flag < 2.0, position, FAR)
            mine = lax.broadcasted_iota(jnp.int32, (1, step), 1) + start
            best = jnp.max(jnp.where(position < mine, gram, -1.0), axis=0, keepdims=True)
            for lane in range(0, step, LANES):
                row = (c * slots + start + lane) // LANES
                res[row:row + 1, :] = best[:, lane:lane + LANES]

    def back_copy(k):
        return pltpu.make_async_remote_copy(
            src_ref=res,
            dst_ref=ret.at[me],
            send_sem=back_send_sem.at[k],
            recv_sem=back_recv_sem.at[k],
            device_id={"wide": peer(k)},
            device_id_type=pl.DeviceIdType.MESH,
        )

    def give_back(k, carry):
        back_copy(k).start()
        return carry

    lax.fori_loop(1, n, give_back, 0)
    ret[me] = res[...]

    def sent(k, carry):
        block_copy(k, 0).wait_send()
        return carry

    lax.fori_loop(1, n, sent, 0)

    def returned(k, carry):
        pltpu.make_async_remote_copy(
            src_ref=res,
            dst_ref=ret.at[lax.rem(me + n - k, n)],
            send_sem=back_send_sem.at[k],
            recv_sem=back_recv_sem.at[k],
            device_id={"wide": peer(k)},
            device_id_type=pl.DeviceIdType.MESH,
        ).wait()
        return carry

    lax.fori_loop(1, n, returned, 0)

    lines = clusters * slots // LANES
    value = ret[...].reshape(lines, LANES)
    place = me * cap
    line = cid * (slots // LANES) + lax.div(place, LANES)
    lane = rank + lax.rem(place, LANES)
    chosen = (lax.broadcasted_iota(jnp.int32, (lines, rows), 0) == line)
    chosen = jnp.where(chosen, 1.0, 0.0).astype(jnp.bfloat16)
    looked = jnp.zeros((LANES, rows), jnp.float32)
    for _ in range(3):
        piece = value.astype(jnp.bfloat16)
        looked = looked + lax.dot_general(
            piece, chosen, (((0,), (0,)), ((), ())), preferred_element_type=jnp.float32
        )
        value = value - piece.astype(jnp.float32)
    at_lane = lax.broadcasted_iota(jnp.int32, (LANES, rows), 0) == lane
    out_ref[...] = jnp.sum(jnp.where(at_lane, looked, 0.0), axis=0, keepdims=True)


def by_kernel(embeddings, cluster_id):
    rows, width = embeddings.shape
    n = lax.axis_size("wide")
    cap = 2 * rows // (CLUS_DEV * n)
    lines = CLUS_DEV * n * cap // LANES
    out = pl.pallas_call(
        functools.partial(dispatch_kernel, n, cap),
        out_shape=jax.ShapeDtypeStruct((1, rows), jnp.float32),
        in_specs=[pl.BlockSpec(memory_space=pltpu.VMEM)] * 2,
        out_specs=pl.BlockSpec(memory_space=pltpu.VMEM),
        scratch_shapes=[
            pltpu.VMEM((rows, width), jnp.bfloat16),
            pltpu.VMEM((n, CLUS_DEV * cap, width), jnp.bfloat16),
            pltpu.VMEM((n, CLUS_DEV * cap, width), jnp.bfloat16),
            pltpu.VMEM((lines, LANES), jnp.float32),
            pltpu.VMEM((n, lines, LANES), jnp.float32),
            pltpu.SemaphoreType.DMA((n,)),
            pltpu.SemaphoreType.DMA((n,)),
            pltpu.SemaphoreType.DMA((n,)),
            pltpu.SemaphoreType.DMA((n,)),
        ],
        compiler_params=pltpu.CompilerParams(
            collective_id=0, has_side_effects=True, vmem_limit_bytes=40 << 20
        ),
    )(embeddings, cluster_id.reshape(1, rows))
    return out.reshape(rows)


def by_collectives(embeddings, cluster_id):
    row_count = embeddings.shape[0]
    wide_count = lax.axis_size("wide")
    per_owner = CLUS_DEV
    capacity = 2 * row_count // (per_owner * wide_count)
    cluster_count = per_owner * wide_count
    total_slots = cluster_count * capacity
    cluster_ids = cluster_id[:, 0]
    onehot = (cluster_ids[:, None] == jnp.arange(cluster_count, dtype=jnp.int32)[None, :]).astype(
        jnp.int32
    )
    earlier = jnp.cumsum(onehot, axis=0) - onehot
    place_rank = jnp.sum(earlier * onehot, axis=1)
    slot_index = cluster_ids * capacity + place_rank
    source_row = (
        jnp.zeros((total_slots,), jnp.int32)
        .at[slot_index]
        .set(jnp.arange(row_count, dtype=jnp.int32))
    )
    filled_flags = jnp.zeros((total_slots,), jnp.bfloat16).at[slot_index].set(jnp.bfloat16(1.0))
    packed = embeddings[source_row].reshape(wide_count, per_owner, capacity, embeddings.shape[1])
    flag_blocks = filled_flags.reshape(wide_count, per_owner, capacity)
    received = lax.all_to_all(packed, "wide", split_axis=0, concat_axis=2, tiled=True)
    flags_here = lax.all_to_all(flag_blocks, "wide", split_axis=0, concat_axis=2, tiled=True)
    unit = normalize(received)
    slot_total = unit.shape[2]
    live = flags_here > 0
    gram = jnp.einsum("pksd,pktd->pkst", unit, unit, preferred_element_type=jnp.float32)
    positions = jnp.arange(slot_total, dtype=jnp.int32)
    mask = (positions[None, :] < positions[:, None])[None, None] & live[:, :, None, :]
    maxima = jnp.max(jnp.where(mask, gram, jnp.float32(-1.0)), axis=3)
    returned = lax.all_to_all(maxima, "wide", split_axis=2, concat_axis=0, tiled=True)
    return returned.reshape(total_slots)[slot_index]


def per_device(embeddings, cluster_id):
    rows, width = embeddings.shape
    n = lax.axis_size("wide")
    cap = 2 * rows // (CLUS_DEV * n)
    if cap % 16 == 0 and n % 4 == 0 and (n * cap) % 256 == 0 and 256 % cap == 0 and width % LANES == 0:
        return by_kernel(embeddings, cluster_id)
    return by_collectives(embeddings, cluster_id)


def solution(mesh):
    in_specs = (P(("parts", "wide"), None), P(("parts", "wide"), None))
    out_specs = P(("parts", "wide"))
    return jax.shard_map(
        per_device, mesh=mesh, in_specs=in_specs, out_specs=out_specs, check_vma=False
    )
```

```python
import functools

import jax
import jax.numpy as jnp
from jax import lax
from jax.experimental import pallas as pl
from jax.experimental.pallas import tpu as pltpu
from jax.sharding import PartitionSpec as P

CLUS_DEV = 2
LANES = 128
EMPTY = 1024.0
CHUNKS = 4
FAR = 1 << 20


def normalize(values):
    widened = values.astype(jnp.float32)
    scale = lax.rsqrt(jnp.sum(widened * widened, axis=-1, keepdims=True) + 1e-06)
    return (widened * scale).astype(jnp.bfloat16)


def ranks(cid, clusters):
    rows = cid.shape[1]
    named = lax.broadcasted_iota(jnp.int32, (clusters, rows), 0) == cid
    before = lax.broadcasted_iota(jnp.int32, (rows, rows), 0) < lax.broadcasted_iota(
        jnp.int32, (rows, rows), 1
    )
    earlier = jnp.dot(
        jnp.where(named, 1.0, 0.0).astype(jnp.bfloat16),
        jnp.where(before, 1.0, 0.0).astype(jnp.bfloat16),
        preferred_element_type=jnp.float32,
    )
    return jnp.sum(jnp.where(named, earlier, 0.0), axis=0, keepdims=True).astype(jnp.int32)


def dispatch_kernel(
    n, cap, emb_ref, cid_ref, out_ref, stage, ids, send, recv, res, ret, picked,
    local_sem, move_send_sem, move_recv_sem, id_sem, send_sem, recv_sem, back_send_sem,
    back_recv_sem,
):
    part = lax.axis_index("parts")
    wide = lax.axis_index("wide")
    half = n // 2
    side = lax.div(wide, half)
    spot = lax.rem(wide, half)
    core = lax.rem(wide, 2)
    away = lax.rem(part + side + 1, 2)
    home = 1 - away
    me = part * half + spot
    guest = 1 - side
    keeps = (home == 1) & (core == 0)
    crosses = lax.rem(home + core, 2) == 1
    rows, width = emb_ref.shape
    block = CLUS_DEV * cap
    slots = n * cap
    clusters = CLUS_DEV * n

    def device(part_of, wide_of):
        return {"parts": part_of, "wide": wide_of}

    def in_cube(index):
        return device(lax.div(index, half), side * half + lax.rem(index, half))

    def block_of(index):
        x, t = lax.div(index, half), lax.rem(index, half)
        flip = lax.rem(x + side + 1 + lax.rem(t, 2), 2)
        return lax.rem(side + flip, 2) * half + t

    def peer(k):
        return lax.rem(me + k, n)

    barrier = pltpu.get_barrier_semaphore()
    everyone = 2 * n

    def greet(k, carry):
        other = lax.rem(part * n + wide + k, everyone)
        pl.semaphore_signal(
            barrier,
            inc=1,
            device_id=device(lax.div(other, n), lax.rem(other, n)),
            device_id_type=pl.DeviceIdType.MESH,
        )
        return carry

    lax.fori_loop(1, everyone, greet, 0)
    own_ids = pltpu.make_async_copy(cid_ref, ids.at[0], local_sem.at[0])
    own_rows = pltpu.make_async_copy(emb_ref, stage.at[0], local_sem.at[1])
    own_ids.start()
    own_rows.start()
    own_ids.wait()
    own_rows.wait()
    own_cid = ids[0]
    own_rank = ranks(own_cid, clusters)

    chunk = rows // CHUNKS
    next_part = jnp.where(crosses, part, 1 - part)
    next_wide = jnp.where(crosses, (1 - side) * half + spot, wide)

    def move(q, source):
        piece = pl.ds(q * chunk, chunk)
        return pltpu.make_async_remote_copy(
            src_ref=stage.at[source, piece],
            dst_ref=stage.at[1, piece],
            send_sem=move_send_sem.at[q],
            recv_sem=move_recv_sem.at[q],
            device_id=device(next_part, next_wide),
            device_id_type=pl.DeviceIdType.MESH,
        )

    def move_ids(source):
        return pltpu.make_async_remote_copy(
            src_ref=ids.at[source],
            dst_ref=ids.at[1],
            send_sem=id_sem.at[0],
            recv_sem=id_sem.at[1],
            device_id=device(next_part, next_wide),
            device_id_type=pl.DeviceIdType.MESH,
        )

    pl.semaphore_wait(barrier, everyone - 1)

    @pl.when(jnp.logical_not(keeps))
    def _():
        move_ids(0).start()
        for q in range(CHUNKS):
            move(q, 0).start()
        move_ids(0).wait_recv()
        for q in range(CHUNKS):
            move(q, 0).wait_recv()

    held = jnp.where(keeps, 0, 1)
    cid = ids[held]
    slot = cid * cap + ranks(cid, clusters)
    place = block_of(me)

    def block_copy(k):
        return pltpu.make_async_remote_copy(
            src_ref=send.at[k],
            dst_ref=recv.at[place],
            send_sem=send_sem.at[k],
            recv_sem=recv_sem.at[k],
            device_id=in_cube(peer(k)),
            device_id_type=pl.DeviceIdType.MESH,
        )

    order = list(range(1, n)) + [0]
    group = 4
    for first in range(0, n, group):
        chosen = order[first:first + group]
        picks = jnp.concatenate(
            [
                jnp.where(
                    lax.broadcasted_iota(jnp.int32, (block, rows), 0) + peer(k) * block == slot,
                    1.0,
                    0.0,
                )
                for k in chosen
            ],
            axis=0,
        )
        packed = jnp.dot(
            picks.astype(jnp.bfloat16), stage[held], preferred_element_type=jnp.float32
        ).astype(jnp.bfloat16)
        filled = jnp.max(picks, axis=1, keepdims=True)
        head = packed[:, :LANES].astype(jnp.float32)
        marked = (lax.broadcasted_iota(jnp.int32, head.shape, 1) == 0) & (filled < 0.5)
        head = jnp.where(marked, EMPTY, head).astype(jnp.bfloat16)
        for i, k in enumerate(chosen):
            piece = slice(i * block, (i + 1) * block)
            if k == 0:
                recv[place, :, :LANES] = head[piece]
                recv[place, :, LANES:] = packed[piece, LANES:]
            else:
                send[k, :, :LANES] = head[piece]
                send[k, :, LANES:] = packed[piece, LANES:]
                block_copy(k).start()

    @pl.when(keeps)
    def _():
        move_ids(1).wait_recv()
        move_ids(1).start()
        for q in range(CHUNKS):
            move(q, 1).wait_recv()
            move(q, 1).start()

    lines = clusters * slots // LANES
    line = own_cid * (slots // LANES) + lax.div(wide * cap, LANES)
    lane = own_rank + lax.rem(wide * cap, LANES)
    own_line = lax.broadcasted_iota(jnp.int32, (lines, rows), 0) == line
    picked[...] = jnp.where(own_line, 1.0, 0.0).astype(jnp.bfloat16)

    def arrived(i, carry):
        kind = lax.div(i, half // 2)
        core_of = lax.rem(lax.div(kind + 1, 2), 2)
        x = lax.rem(guest + lax.rem(kind, 2), 2)
        index = x * half + lax.rem(i, half // 2) * 2 + core_of
        k = lax.rem(me - index + n, n)
        came = block_of(index)

        @pl.when(k != 0)
        def _():
            pltpu.make_async_remote_copy(
                src_ref=send.at[0],
                dst_ref=recv.at[came],
                send_sem=send_sem.at[k],
                recv_sem=recv_sem.at[k],
                device_id=in_cube(index),
                device_id_type=pl.DeviceIdType.MESH,
            ).wait_recv()

        raw = recv[came]
        unit = normalize(raw)
        head = unit[:, :LANES].astype(jnp.float32)
        first = lax.broadcasted_iota(jnp.int32, head.shape, 1) == 0
        marked = first & (raw[:, :LANES].astype(jnp.float32) > EMPTY / 2)
        recv[came, :, :LANES] = jnp.where(marked, EMPTY, head).astype(jnp.bfloat16)
        recv[came, :, LANES:] = unit[:, LANES:]
        return carry

    lax.fori_loop(0, n, arrived, 0)

    step = 256
    for c in range(CLUS_DEV):
        for start in range(0, slots, step):
            top = start + step
            keys = recv[: top // cap, c * cap:(c + 1) * cap, :].reshape(top, width)
            queries = recv[start // cap:top // cap, c * cap:(c + 1) * cap, :].reshape(step, width)
            gram = lax.dot_general(
                keys, queries, (((1,), (1,)), ((), ())), preferred_element_type=jnp.float32
            )
            flag = keys[:, :LANES].astype(jnp.float32)[:, :1]
            position = lax.broadcasted_iota(jnp.int32, (top, 1), 0)
            position = jnp.where(flag < 2.0, position, FAR)
            mine = lax.broadcasted_iota(jnp.int32, (1, step), 1) + start
            best = jnp.max(jnp.where(position < mine, gram, -1.0), axis=0, keepdims=True)
            for at in range(0, step, LANES):
                row = (c * slots + start + at) // LANES
                res[row:row + 1, :] = best[:, at:at + LANES]

    def back_copy(k):
        return pltpu.make_async_remote_copy(
            src_ref=res,
            dst_ref=ret.at[me],
            send_sem=back_send_sem.at[k],
            recv_sem=back_recv_sem.at[me],
            device_id=device(guest, lax.rem(wide + k, n)),
            device_id_type=pl.DeviceIdType.MESH,
        )

    def give_back(k, carry):
        back_copy(k).start()
        return carry

    lax.fori_loop(home, n, give_back, 0)

    @pl.when(home == 1)
    def _():
        ret[me] = res[...]

    move_ids(0).wait_send()
    for q in range(CHUNKS):
        move(q, 0).wait_send()

    def sent(k, carry):
        block_copy(k).wait_send()
        return carry

    lax.fori_loop(1, n, sent, 0)

    def given(k, carry):
        back_copy(k).wait_send()
        return carry

    lax.fori_loop(home, n, given, 0)

    def returned(index, carry):
        @pl.when((home == 0) | (index != me))
        def _():
            pltpu.make_async_remote_copy(
                src_ref=res,
                dst_ref=ret.at[index],
                send_sem=back_send_sem.at[0],
                recv_sem=back_recv_sem.at[index],
                device_id=device(guest, lax.rem(wide + 1, n)),
                device_id_type=pl.DeviceIdType.MESH,
            ).wait_recv()

        return carry

    lax.fori_loop(0, n, returned, 0)

    value = ret[...].reshape(lines, LANES)
    looked = jnp.zeros((LANES, rows), jnp.float32)
    for _ in range(3):
        piece = value.astype(jnp.bfloat16)
        looked = looked + lax.dot_general(
            piece, picked[...], (((0,), (0,)), ((), ())), preferred_element_type=jnp.float32
        )
        value = value - piece.astype(jnp.float32)
    at_lane = lax.broadcasted_iota(jnp.int32, (LANES, rows), 0) == lane
    out_ref[...] = jnp.sum(jnp.where(at_lane, looked, 0.0), axis=0, keepdims=True)


def by_kernel(embeddings, cluster_id):
    rows, width = embeddings.shape
    n = lax.axis_size("wide")
    cap = 2 * rows // (CLUS_DEV * n)
    lines = CLUS_DEV * n * cap // LANES
    out = pl.pallas_call(
        functools.partial(dispatch_kernel, n, cap),
        out_shape=jax.ShapeDtypeStruct((1, rows), jnp.float32),
        in_specs=[pl.BlockSpec(memory_space=pl.ANY)] * 2,
        out_specs=pl.BlockSpec(memory_space=pltpu.VMEM),
        scratch_shapes=[
            pltpu.VMEM((2, rows, width), jnp.bfloat16),
            pltpu.VMEM((2, 1, rows), jnp.int32),
            pltpu.VMEM((n, CLUS_DEV * cap, width), jnp.bfloat16),
            pltpu.VMEM((n, CLUS_DEV * cap, width), jnp.bfloat16),
            pltpu.VMEM((lines, LANES), jnp.float32),
            pltpu.VMEM((n, lines, LANES), jnp.float32),
            pltpu.VMEM((n * lines, rows), jnp.bfloat16),
            pltpu.SemaphoreType.DMA((2,)),
            pltpu.SemaphoreType.DMA((CHUNKS,)),
            pltpu.SemaphoreType.DMA((CHUNKS,)),
            pltpu.SemaphoreType.DMA((2,)),
            pltpu.SemaphoreType.DMA((n,)),
            pltpu.SemaphoreType.DMA((n,)),
            pltpu.SemaphoreType.DMA((n,)),
            pltpu.SemaphoreType.DMA((n,)),
        ],
        compiler_params=pltpu.CompilerParams(
            collective_id=0, has_side_effects=True, vmem_limit_bytes=56 << 20
        ),
    )(embeddings, cluster_id.reshape(1, rows))
    return out.reshape(rows)


def by_collectives(embeddings, cluster_id):
    row_count = embeddings.shape[0]
    wide_count = lax.axis_size("wide")
    per_owner = CLUS_DEV
    capacity = 2 * row_count // (per_owner * wide_count)
    cluster_count = per_owner * wide_count
    total_slots = cluster_count * capacity
    cluster_ids = cluster_id[:, 0]
    onehot = (cluster_ids[:, None] == jnp.arange(cluster_count, dtype=jnp.int32)[None, :]).astype(
        jnp.int32
    )
    earlier = jnp.cumsum(onehot, axis=0) - onehot
    place_rank = jnp.sum(earlier * onehot, axis=1)
    slot_index = cluster_ids * capacity + place_rank
    source_row = (
        jnp.zeros((total_slots,), jnp.int32)
        .at[slot_index]
        .set(jnp.arange(row_count, dtype=jnp.int32))
    )
    filled_flags = jnp.zeros((total_slots,), jnp.bfloat16).at[slot_index].set(jnp.bfloat16(1.0))
    packed = embeddings[source_row].reshape(wide_count, per_owner, capacity, embeddings.shape[1])
    flag_blocks = filled_flags.reshape(wide_count, per_owner, capacity)
    received = lax.all_to_all(packed, "wide", split_axis=0, concat_axis=2, tiled=True)
    flags_here = lax.all_to_all(flag_blocks, "wide", split_axis=0, concat_axis=2, tiled=True)
    unit = normalize(received)
    slot_total = unit.shape[2]
    live = flags_here > 0
    gram = jnp.einsum("pksd,pktd->pkst", unit, unit, preferred_element_type=jnp.float32)
    positions = jnp.arange(slot_total, dtype=jnp.int32)
    mask = (positions[None, :] < positions[:, None])[None, None] & live[:, :, None, :]
    maxima = jnp.max(jnp.where(mask, gram, jnp.float32(-1.0)), axis=3)
    returned = lax.all_to_all(maxima, "wide", split_axis=2, concat_axis=0, tiled=True)
    return returned.reshape(total_slots)[slot_index]


def per_device(embeddings, cluster_id):
    rows, width = embeddings.shape
    n = lax.axis_size("wide")
    cap = 2 * rows // (CLUS_DEV * n)
    if lax.axis_size("parts") == 2 and n == 16 and cap == 32 and width % LANES == 0:
        return by_kernel(embeddings, cluster_id)
    return by_collectives(embeddings, cluster_id)


def solution(mesh):
    in_specs = (P(("parts", "wide"), None), P(("parts", "wide"), None))
    out_specs = P(("parts", "wide"))
    return jax.shard_map(
        per_device, mesh=mesh, in_specs=in_specs, out_specs=out_specs, check_vma=False
    )
```

```python
import functools

import jax
import jax.numpy as jnp
from jax import lax
from jax.experimental import pallas as pl
from jax.experimental.pallas import tpu as pltpu
from jax.sharding import PartitionSpec as P

CLUS_DEV = 2
LANES = 128
EMPTY = 4.0
FAR = 1 << 20
GROUPS = (4, 4, 4, 4)
EARLY = 4


def normalize(values):
    widened = values.astype(jnp.float32)
    scale = lax.rsqrt(jnp.sum(widened * widened, axis=-1, keepdims=True) + 1e-06)
    return (widened * scale).astype(jnp.bfloat16)


def dispatch_kernel(
    n, cap, emb_ref, cid_ref, out_ref, rows_here, ids, before, send, recv, res, ret, picked,
    local_sem, send_sem, recv_sem, back_send_sem, back_recv_sem,
):
    me = lax.axis_index("wide")
    half = n // 2
    side = lax.div(me, half)
    spot = lax.rem(me, half)
    rows, width = emb_ref.shape
    block = CLUS_DEV * cap
    slots = n * cap
    clusters = CLUS_DEV * n

    def peer(k):
        base = jnp.where(k < half, 1 - side, side) * half
        return base + lax.rem(spot + lax.rem(k, half), half)

    def source(k):
        base = jnp.where(k < half, 1 - side, side) * half
        return base + lax.rem(spot + half - lax.rem(k, half), half)

    def partners(body):
        lax.fori_loop(0, half, body, 0)
        lax.fori_loop(half + 1, n, body, 0)

    get_ids = pltpu.make_async_copy(cid_ref, ids, local_sem.at[0])
    get_rows = pltpu.make_async_copy(emb_ref, rows_here, local_sem.at[1])
    get_ids.start()
    get_rows.start()

    barrier = pltpu.get_barrier_semaphore()

    def greet(k, carry):
        pl.semaphore_signal(
            barrier, inc=1, device_id={"wide": peer(k)}, device_id_type=pl.DeviceIdType.MESH
        )
        return carry

    partners(greet)

    earlier_row = lax.broadcasted_iota(jnp.int32, (rows, rows), 0) < lax.broadcasted_iota(
        jnp.int32, (rows, rows), 1
    )
    before[...] = jnp.where(earlier_row, 1.0, 0.0).astype(jnp.bfloat16)
    get_ids.wait()
    cid = ids[...]
    named = lax.broadcasted_iota(jnp.int32, (clusters, rows), 0) == cid
    earlier = jnp.dot(
        jnp.where(named, 1.0, 0.0).astype(jnp.bfloat16),
        before[...],
        preferred_element_type=jnp.float32,
    )
    rank = jnp.sum(jnp.where(named, earlier, 0.0), axis=0, keepdims=True).astype(jnp.int32)
    slot = cid * cap + rank

    get_rows.wait()

    def block_copy(k, place):
        return pltpu.make_async_remote_copy(
            src_ref=send.at[place],
            dst_ref=recv.at[me],
            send_sem=send_sem.at[k],
            recv_sem=recv_sem.at[k],
            device_id={"wide": peer(k)},
            device_id_type=pl.DeviceIdType.MESH,
        )

    order = [0]
    for k in range(1, half):
        order += [half + k, k]
    order.append(half)
    first = 0
    for group in GROUPS:
        chosen = order[first:first + group]
        picks = jnp.concatenate(
            [
                jnp.where(
                    lax.broadcasted_iota(jnp.int32, (block, rows), 0) + peer(k) * block == slot,
                    1.0,
                    0.0,
                )
                for k in chosen
            ],
            axis=0,
        )
        packed = jnp.dot(
            picks.astype(jnp.bfloat16), rows_here[...], preferred_element_type=jnp.float32
        )
        packed = normalize(packed)
        filled = jnp.max(picks, axis=1, keepdims=True)
        head = packed[:, :LANES].astype(jnp.float32)
        marked = (lax.broadcasted_iota(jnp.int32, head.shape, 1) == 0) & (filled < 0.5)
        head = jnp.where(marked, EMPTY, head).astype(jnp.bfloat16)
        for i, k in enumerate(chosen):
            part = slice(i * block, (i + 1) * block)
            if k == half:
                recv[me, :, :LANES] = head[part]
                recv[me, :, LANES:] = packed[part, LANES:]
            else:
                send[first + i, :, :LANES] = head[part]
                send[first + i, :, LANES:] = packed[part, LANES:]
        first += group
        if first == EARLY:
            pl.semaphore_wait(barrier, n - 1)
            for i, k in enumerate(order[:first]):
                block_copy(k, i).start()
        elif first > EARLY:
            for i, k in enumerate(chosen):
                if k != half:
                    block_copy(k, first - group + i).start()

    lines = clusters * slots // LANES
    place = me * cap
    line = cid * (slots // LANES) + lax.div(place, LANES)
    lane = rank + lax.rem(place, LANES)
    own_line = lax.broadcasted_iota(jnp.int32, (lines, rows), 0) == line
    picked[...] = jnp.where(own_line, 1.0, 0.0).astype(jnp.bfloat16)

    def arrived(k, carry):
        pltpu.make_async_remote_copy(
            src_ref=send.at[0],
            dst_ref=recv.at[source(k)],
            send_sem=send_sem.at[k],
            recv_sem=recv_sem.at[k],
            device_id={"wide": peer(k)},
            device_id_type=pl.DeviceIdType.MESH,
        ).wait_recv()
        return carry

    step = slots // 2

    def largest(c, k, q, within):
        def slots_of(h):
            blocks = recv[pl.ds(h * half, half), c * cap:(c + 1) * cap, :]
            return blocks.reshape(step, width)

        keys = slots_of(k)
        gram = lax.dot_general(
            keys, slots_of(q), (((1,), (1,)), ((), ())), preferred_element_type=jnp.float32
        )
        flag = keys[:, :LANES].astype(jnp.float32)[:, :1]
        position = lax.broadcasted_iota(jnp.int32, (step, 1), 0) if within else 0
        position = jnp.where(flag < 2.0, position, FAR)
        mine = lax.broadcasted_iota(jnp.int32, (1, step), 1) if within else 1
        return jnp.max(jnp.where(position < mine, gram, -1.0), axis=0, keepdims=True)

    def within_half(h):
        for c in range(CLUS_DEV):
            best = largest(c, h, h, True)
            for i in range(step // LANES):
                row = (c * slots + h * step) // LANES + i
                res[pl.ds(row, 1), :] = best[:, i * LANES:(i + 1) * LANES]

    lax.fori_loop(half + 1, n, arrived, 0)
    within_half(side)
    lax.fori_loop(0, half, arrived, 0)
    within_half(1 - side)
    for c in range(CLUS_DEV):
        best = largest(c, 0, 1, False)
        for i in range(step // LANES):
            row = (c * slots + step) // LANES + i
            res[row:row + 1, :] = jnp.maximum(
                res[row:row + 1, :], best[:, i * LANES:(i + 1) * LANES]
            )

    def back_copy(k):
        return pltpu.make_async_remote_copy(
            src_ref=res,
            dst_ref=ret.at[me],
            send_sem=back_send_sem.at[k],
            recv_sem=back_recv_sem.at[k],
            device_id={"wide": peer(k)},
            device_id_type=pl.DeviceIdType.MESH,
        )

    def give_back(k, carry):
        back_copy(k).start()
        return carry

    partners(give_back)
    ret[me] = res[...]

    def sent(k, carry):
        block_copy(k, 0).wait_send()
        return carry

    partners(sent)

    def returned(k, carry):
        pltpu.make_async_remote_copy(
            src_ref=res,
            dst_ref=ret.at[source(k)],
            send_sem=back_send_sem.at[k],
            recv_sem=back_recv_sem.at[k],
            device_id={"wide": peer(k)},
            device_id_type=pl.DeviceIdType.MESH,
        ).wait()
        return carry

    partners(returned)

    value = ret[...].reshape(lines, LANES)
    looked = jnp.zeros((LANES, rows), jnp.float32)
    for _ in range(3):
        piece = value.astype(jnp.bfloat16)
        looked = looked + lax.dot_general(
            piece, picked[...], (((0,), (0,)), ((), ())), preferred_element_type=jnp.float32
        )
        value = value - piece.astype(jnp.float32)
    at_lane = lax.broadcasted_iota(jnp.int32, (LANES, rows), 0) == lane
    out_ref[...] = jnp.sum(jnp.where(at_lane, looked, 0.0), axis=0, keepdims=True)


def by_kernel(embeddings, cluster_id):
    rows, width = embeddings.shape
    n = lax.axis_size("wide")
    cap = 2 * rows // (CLUS_DEV * n)
    lines = CLUS_DEV * n * cap // LANES
    out = pl.pallas_call(
        functools.partial(dispatch_kernel, n, cap),
        out_shape=jax.ShapeDtypeStruct((1, rows), jnp.float32),
        in_specs=[pl.BlockSpec(memory_space=pl.ANY)] * 2,
        out_specs=pl.BlockSpec(memory_space=pltpu.VMEM),
        scratch_shapes=[
            pltpu.VMEM((rows, width), jnp.bfloat16),
            pltpu.VMEM((1, rows), jnp.int32),
            pltpu.VMEM((rows, rows), jnp.bfloat16),
            pltpu.VMEM((n, CLUS_DEV * cap, width), jnp.bfloat16),
            pltpu.VMEM((n, CLUS_DEV * cap, width), jnp.bfloat16),
            pltpu.VMEM((lines, LANES), jnp.float32),
            pltpu.VMEM((n, lines, LANES), jnp.float32),
            pltpu.VMEM((n * lines, rows), jnp.bfloat16),
            pltpu.SemaphoreType.DMA((2,)),
            pltpu.SemaphoreType.DMA((n,)),
            pltpu.SemaphoreType.DMA((n,)),
            pltpu.SemaphoreType.DMA((n,)),
            pltpu.SemaphoreType.DMA((n,)),
        ],
        compiler_params=pltpu.CompilerParams(
            collective_id=0, has_side_effects=True, vmem_limit_bytes=56 << 20
        ),
    )(embeddings, cluster_id.reshape(1, rows))
    return out.reshape(rows)


def by_collectives(embeddings, cluster_id):
    row_count = embeddings.shape[0]
    wide_count = lax.axis_size("wide")
    per_owner = CLUS_DEV
    capacity = 2 * row_count // (per_owner * wide_count)
    cluster_count = per_owner * wide_count
    total_slots = cluster_count * capacity
    cluster_ids = cluster_id[:, 0]
    onehot = (cluster_ids[:, None] == jnp.arange(cluster_count, dtype=jnp.int32)[None, :]).astype(
        jnp.int32
    )
    earlier = jnp.cumsum(onehot, axis=0) - onehot
    place_rank = jnp.sum(earlier * onehot, axis=1)
    slot_index = cluster_ids * capacity + place_rank
    source_row = (
        jnp.zeros((total_slots,), jnp.int32)
        .at[slot_index]
        .set(jnp.arange(row_count, dtype=jnp.int32))
    )
    filled_flags = jnp.zeros((total_slots,), jnp.bfloat16).at[slot_index].set(jnp.bfloat16(1.0))
    packed = embeddings[source_row].reshape(wide_count, per_owner, capacity, embeddings.shape[1])
    flag_blocks = filled_flags.reshape(wide_count, per_owner, capacity)
    received = lax.all_to_all(packed, "wide", split_axis=0, concat_axis=2, tiled=True)
    flags_here = lax.all_to_all(flag_blocks, "wide", split_axis=0, concat_axis=2, tiled=True)
    unit = normalize(received)
    slot_total = unit.shape[2]
    live = flags_here > 0
    gram = jnp.einsum("pksd,pktd->pkst", unit, unit, preferred_element_type=jnp.float32)
    positions = jnp.arange(slot_total, dtype=jnp.int32)
    mask = (positions[None, :] < positions[:, None])[None, None] & live[:, :, None, :]
    maxima = jnp.max(jnp.where(mask, gram, jnp.float32(-1.0)), axis=3)
    returned = lax.all_to_all(maxima, "wide", split_axis=2, concat_axis=0, tiled=True)
    return returned.reshape(total_slots)[slot_index]


def per_device(embeddings, cluster_id):
    rows, width = embeddings.shape
    n = lax.axis_size("wide")
    cap = 2 * rows // (CLUS_DEV * n)
    if n == 16 and cap == 32 and width % LANES == 0:
        return by_kernel(embeddings, cluster_id)
    return by_collectives(embeddings, cluster_id)


def solution(mesh):
    in_specs = (P(("parts", "wide"), None), P(("parts", "wide"), None))
    out_specs = P(("parts", "wide"))
    return jax.shard_map(
        per_device, mesh=mesh, in_specs=in_specs, out_specs=out_specs, check_vma=False
    )
```

```python
import functools

import jax
import jax.numpy as jnp
from jax import lax
from jax.experimental import pallas as pl
from jax.experimental.pallas import tpu as pltpu
from jax.sharding import PartitionSpec as P

CLUS_DEV = 2
LANES = 128
EMPTY = 4.0
FAR = 1 << 20
GROUPS = (4, 4, 4, 4)
EARLY = 4


def normalize(values):
    widened = values.astype(jnp.float32)
    scale = lax.rsqrt(jnp.sum(widened * widened, axis=-1, keepdims=True) + 1e-06)
    return (widened * scale).astype(jnp.bfloat16)


def dispatch_kernel(
    n, cap, emb_ref, cid_ref, out_ref, rows_here, ids, before, send, recv, res, ret, picked,
    local_sem, send_sem, recv_sem, back_send_sem, back_recv_sem,
):
    me = lax.axis_index("wide")
    half = n // 2
    side = lax.div(me, half)
    spot = lax.rem(me, half)
    rows, width = emb_ref.shape
    block = CLUS_DEV * cap
    slots = n * cap
    clusters = CLUS_DEV * n

    def peer(k):
        base = jnp.where(k < half, 1 - side, side) * half
        return base + lax.rem(spot + lax.rem(k, half), half)

    def source(k):
        base = jnp.where(k < half, 1 - side, side) * half
        return base + lax.rem(spot + half - lax.rem(k, half), half)

    def partners(body):
        lax.fori_loop(0, half, body, 0)
        lax.fori_loop(half + 1, n, body, 0)

    get_ids = pltpu.make_async_copy(cid_ref, ids, local_sem.at[0])
    get_rows = pltpu.make_async_copy(emb_ref, rows_here, local_sem.at[1])
    get_ids.start()
    get_rows.start()

    barrier = pltpu.get_barrier_semaphore()

    def greet(k, carry):
        pl.semaphore_signal(
            barrier, inc=1, device_id={"wide": peer(k)}, device_id_type=pl.DeviceIdType.MESH
        )
        return carry

    partners(greet)

    earlier_row = lax.broadcasted_iota(jnp.int32, (rows, rows), 0) < lax.broadcasted_iota(
        jnp.int32, (rows, rows), 1
    )
    before[...] = jnp.where(earlier_row, 1.0, 0.0).astype(jnp.bfloat16)
    get_ids.wait()
    cid = ids[...]
    named = lax.broadcasted_iota(jnp.int32, (clusters, rows), 0) == cid
    earlier = jnp.dot(
        jnp.where(named, 1.0, 0.0).astype(jnp.bfloat16),
        before[...],
        preferred_element_type=jnp.float32,
    )
    rank = jnp.sum(jnp.where(named, earlier, 0.0), axis=0, keepdims=True).astype(jnp.int32)
    slot = cid * cap + rank

    get_rows.wait()

    def block_copy(k, place):
        return pltpu.make_async_remote_copy(
            src_ref=send.at[place],
            dst_ref=recv.at[me],
            send_sem=send_sem.at[k],
            recv_sem=recv_sem.at[k],
            device_id={"wide": peer(k)},
            device_id_type=pl.DeviceIdType.MESH,
        )

    order = [0]
    for k in range(1, half):
        order += [half + k, k]
    order.append(half)
    first = 0
    for group in GROUPS:
        chosen = order[first:first + group]
        picks = jnp.concatenate(
            [
                jnp.where(
                    lax.broadcasted_iota(jnp.int32, (block, rows), 0) + peer(k) * block == slot,
                    1.0,
                    0.0,
                )
                for k in chosen
            ],
            axis=0,
        )
        packed = jnp.dot(
            picks.astype(jnp.bfloat16), rows_here[...], preferred_element_type=jnp.float32
        )
        packed = normalize(packed)
        filled = jnp.max(picks, axis=1, keepdims=True)
        head = packed[:, :LANES].astype(jnp.float32)
        marked = (lax.broadcasted_iota(jnp.int32, head.shape, 1) == 0) & (filled < 0.5)
        head = jnp.where(marked, EMPTY, head).astype(jnp.bfloat16)
        for i, k in enumerate(chosen):
            part = slice(i * block, (i + 1) * block)
            if k == half:
                recv[me, :, :LANES] = head[part]
                recv[me, :, LANES:] = packed[part, LANES:]
            else:
                send[first + i, :, :LANES] = head[part]
                send[first + i, :, LANES:] = packed[part, LANES:]
        first += group
        if first == EARLY:
            pl.semaphore_wait(barrier, n - 1)
            for i, k in enumerate(order[:first]):
                block_copy(k, i).start()
        elif first > EARLY:
            for i, k in enumerate(chosen):
                if k != half:
                    if k < half and k >= 5:
                        block_copy(k - 5, 0).wait_send()
                    block_copy(k, first - group + i).start()

    lines = clusters * slots // LANES
    place = me * cap
    line = cid * (slots // LANES) + lax.div(place, LANES)
    lane = rank + lax.rem(place, LANES)
    own_line = lax.broadcasted_iota(jnp.int32, (lines, rows), 0) == line
    picked[...] = jnp.where(own_line, 1.0, 0.0).astype(jnp.bfloat16)

    def arrived(k, carry):
        pltpu.make_async_remote_copy(
            src_ref=send.at[0],
            dst_ref=recv.at[source(k)],
            send_sem=send_sem.at[k],
            recv_sem=recv_sem.at[k],
            device_id={"wide": peer(k)},
            device_id_type=pl.DeviceIdType.MESH,
        ).wait_recv()
        return carry

    step = slots // 2

    def largest(c, k, q, within):
        def slots_of(h):
            blocks = recv[pl.ds(h * half, half), c * cap:(c + 1) * cap, :]
            return blocks.reshape(step, width)

        keys = slots_of(k)
        gram = lax.dot_general(
            keys, slots_of(q), (((1,), (1,)), ((), ())), preferred_element_type=jnp.float32
        )
        flag = keys[:, :LANES].astype(jnp.float32)[:, :1]
        position = lax.broadcasted_iota(jnp.int32, (step, 1), 0) if within else 0
        position = jnp.where(flag < 2.0, position, FAR)
        mine = lax.broadcasted_iota(jnp.int32, (1, step), 1) if within else 1
        return jnp.max(jnp.where(position < mine, gram, -1.0), axis=0, keepdims=True)

    def within_half(h):
        for c in range(CLUS_DEV):
            best = largest(c, h, h, True)
            for i in range(step // LANES):
                row = (c * slots + h * step) // LANES + i
                res[pl.ds(row, 1), :] = best[:, i * LANES:(i + 1) * LANES]

    lax.fori_loop(half + 1, n, arrived, 0)
    within_half(side)
    lax.fori_loop(0, half, arrived, 0)
    within_half(1 - side)
    for c in range(CLUS_DEV):
        best = largest(c, 0, 1, False)
        for i in range(step // LANES):
            row = (c * slots + step) // LANES + i
            res[row:row + 1, :] = jnp.maximum(
                res[row:row + 1, :], best[:, i * LANES:(i + 1) * LANES]
            )

    def back_copy(k):
        return pltpu.make_async_remote_copy(
            src_ref=res,
            dst_ref=ret.at[me],
            send_sem=back_send_sem.at[k],
            recv_sem=back_recv_sem.at[k],
            device_id={"wide": peer(k)},
            device_id_type=pl.DeviceIdType.MESH,
        )

    def give_back(k, carry):
        back_copy(k).start()
        return carry

    partners(give_back)
    ret[me] = res[...]

    def sent(k, carry):
        block_copy(k, 0).wait_send()
        return carry

    lax.fori_loop(3, half, sent, 0)
    lax.fori_loop(half + 1, n, sent, 0)

    def returned(k, carry):
        pltpu.make_async_remote_copy(
            src_ref=res,
            dst_ref=ret.at[source(k)],
            send_sem=back_send_sem.at[k],
            recv_sem=back_recv_sem.at[k],
            device_id={"wide": peer(k)},
            device_id_type=pl.DeviceIdType.MESH,
        ).wait()
        return carry

    partners(returned)

    value = ret[...].reshape(lines, LANES)
    looked = jnp.zeros((LANES, rows), jnp.float32)
    for _ in range(3):
        piece = value.astype(jnp.bfloat16)
        looked = looked + lax.dot_general(
            piece, picked[...], (((0,), (0,)), ((), ())), preferred_element_type=jnp.float32
        )
        value = value - piece.astype(jnp.float32)
    at_lane = lax.broadcasted_iota(jnp.int32, (LANES, rows), 0) == lane
    out_ref[...] = jnp.sum(jnp.where(at_lane, looked, 0.0), axis=0, keepdims=True)


def by_kernel(embeddings, cluster_id):
    rows, width = embeddings.shape
    n = lax.axis_size("wide")
    cap = 2 * rows // (CLUS_DEV * n)
    lines = CLUS_DEV * n * cap // LANES
    out = pl.pallas_call(
        functools.partial(dispatch_kernel, n, cap),
        out_shape=jax.ShapeDtypeStruct((1, rows), jnp.float32),
        in_specs=[pl.BlockSpec(memory_space=pl.ANY)] * 2,
        out_specs=pl.BlockSpec(memory_space=pltpu.VMEM),
        scratch_shapes=[
            pltpu.VMEM((rows, width), jnp.bfloat16),
            pltpu.VMEM((1, rows), jnp.int32),
            pltpu.VMEM((rows, rows), jnp.bfloat16),
            pltpu.VMEM((n, CLUS_DEV * cap, width), jnp.bfloat16),
            pltpu.VMEM((n, CLUS_DEV * cap, width), jnp.bfloat16),
            pltpu.VMEM((lines, LANES), jnp.float32),
            pltpu.VMEM((n, lines, LANES), jnp.float32),
            pltpu.VMEM((n * lines, rows), jnp.bfloat16),
            pltpu.SemaphoreType.DMA((2,)),
            pltpu.SemaphoreType.DMA((n,)),
            pltpu.SemaphoreType.DMA((n,)),
            pltpu.SemaphoreType.DMA((n,)),
            pltpu.SemaphoreType.DMA((n,)),
        ],
        compiler_params=pltpu.CompilerParams(
            collective_id=0, has_side_effects=True, vmem_limit_bytes=56 << 20
        ),
    )(embeddings, cluster_id.reshape(1, rows))
    return out.reshape(rows)


def by_collectives(embeddings, cluster_id):
    row_count = embeddings.shape[0]
    wide_count = lax.axis_size("wide")
    per_owner = CLUS_DEV
    capacity = 2 * row_count // (per_owner * wide_count)
    cluster_count = per_owner * wide_count
    total_slots = cluster_count * capacity
    cluster_ids = cluster_id[:, 0]
    onehot = (cluster_ids[:, None] == jnp.arange(cluster_count, dtype=jnp.int32)[None, :]).astype(
        jnp.int32
    )
    earlier = jnp.cumsum(onehot, axis=0) - onehot
    place_rank = jnp.sum(earlier * onehot, axis=1)
    slot_index = cluster_ids * capacity + place_rank
    source_row = (
        jnp.zeros((total_slots,), jnp.int32)
        .at[slot_index]
        .set(jnp.arange(row_count, dtype=jnp.int32))
    )
    filled_flags = jnp.zeros((total_slots,), jnp.bfloat16).at[slot_index].set(jnp.bfloat16(1.0))
    packed = embeddings[source_row].reshape(wide_count, per_owner, capacity, embeddings.shape[1])
    flag_blocks = filled_flags.reshape(wide_count, per_owner, capacity)
    received = lax.all_to_all(packed, "wide", split_axis=0, concat_axis=2, tiled=True)
    flags_here = lax.all_to_all(flag_blocks, "wide", split_axis=0, concat_axis=2, tiled=True)
    unit = normalize(received)
    slot_total = unit.shape[2]
    live = flags_here > 0
    gram = jnp.einsum("pksd,pktd->pkst", unit, unit, preferred_element_type=jnp.float32)
    positions = jnp.arange(slot_total, dtype=jnp.int32)
    mask = (positions[None, :] < positions[:, None])[None, None] & live[:, :, None, :]
    maxima = jnp.max(jnp.where(mask, gram, jnp.float32(-1.0)), axis=3)
    returned = lax.all_to_all(maxima, "wide", split_axis=2, concat_axis=0, tiled=True)
    return returned.reshape(total_slots)[slot_index]


def per_device(embeddings, cluster_id):
    rows, width = embeddings.shape
    n = lax.axis_size("wide")
    cap = 2 * rows // (CLUS_DEV * n)
    if n == 16 and cap == 32 and width % LANES == 0:
        return by_kernel(embeddings, cluster_id)
    return by_collectives(embeddings, cluster_id)


def solution(mesh):
    in_specs = (P(("parts", "wide"), None), P(("parts", "wide"), None))
    out_specs = P(("parts", "wide"))
    return jax.shard_map(
        per_device, mesh=mesh, in_specs=in_specs, out_specs=out_specs, check_vma=False
    )
```
